32 devices in a mesh: group: 2 (over x), expert: 16 (over z, y, core).
Axes of the slice: x: 2, y: 2, z: 4, core: 2. Of those that a mesh axis runs over, the one named last changes fastest.
Arguments:
- resid: bfloat16 [2048, 4096], P(('group', 'expert')), parts along dimension 0, may hold values from -30 to 30
- queries: bfloat16 [2048, 4096], P(('group', 'expert')), parts along dimension 0, may hold values from -8 to 8
- block_keys: bfloat16 [2048, 512], P(('group', 'expert')), parts along dimension 0, may hold values from -6 to 6
- block_values: bfloat16 [2048, 512], P(('group', 'expert')), parts along dimension 0, may hold values from -6 to 6
- cache_keys: bfloat16 [64, 1024, 512], P(('group', 'expert')), parts along dimension 0, may hold values from -8 to 8
- cache_values: bfloat16 [64, 1024, 512], P(('group', 'expert')), parts along dimension 0, may hold values from -6 to 6
- prefix_len: int32 [64], P(('group', 'expert')), parts along dimension 0, may hold values from 2 to 1024
- norm_gain: float32 [4096], replicated, may hold values from 0.5 to 1.5
- expert_ids: int32 [2048, 4], P(('group', 'expert')), parts along dimension 0, may hold values from 0 to 7, all different within a row; in each aligned block of 64 rows (0 to 63, 64 to 127, ...) at most 48 rows name the same one
- route_weights: float32 [2048, 4], P(('group', 'expert')), parts along dimension 0, may hold values from 0.1 to 1
- w_gate: bfloat16 [16, 4096, 256], P('expert'), may hold values from -0.09375 to 0.09375
- w_up: bfloat16 [16, 4096, 256], P('expert'), may hold values from -0.09375 to 0.09375
- w_down: bfloat16 [16, 256, 4096], P('expert'), may hold values from -0.25 to 0.25
Outputs:
- layer_out: bfloat16 [2048, 4096], P(('group', 'expert')), parts along dimension 0
The draws below stay inside these ranges and needn't reach their ends.
There are 2 independent parts, one for each index of `group`. The reference program is written for one: setup_inputs(seed, part) draws one part's arguments, and reference() takes and returns one part's arrays. A program takes and returns all parts, laid end to end along the dimension named above; an argument that names none is the same for every part. Nothing has to cross between parts.
Inputs may be any that keep to these rules, and one draw needn't show every extreme that they name: `expert_ids`: each row names 4 different experts; in each aligned block of 64 rows (the rows of one device) no expert is named by more than 48 rows, a bound that some block reaches.
All inputs are finite; a program needn't handle non-finite values.
Results may differ from the reference program's by a relative error of at most 0.008.
Values may be sent and summed in bfloat16 or wider, within the bound.
No kernel may reach another device: no remote copies, remote signals or barrier semaphores. Data moves between devices by JAX's collectives and lax.ppermute only.
A program may use at most 128 MiB of HBM per device.

```python
import math
import jax
import jax.numpy as jnp
import numpy as np
from jax import lax

D = 4096
HEADS = 32
KV_HEADS = 4
HEAD_DIM = 128
FF = 512
BLOCK = 32
PREFIX = 1024
EXPERTS = 8
TOPK = 4
TOK_DEV = 64
REQUESTS = 32
TOKENS = 1024
CAP = 48
N_EXPERT = 16


def draw_queries(key, part):
    key = jax.random.fold_in(key, 1)
    values = jnp.clip(jax.random.normal(key, (TOKENS, HEADS * HEAD_DIM)), -8.0, 8.0)
    return values.astype(jnp.bfloat16)


def draw_cache_keys(key, part):
    key = jax.random.fold_in(key, 2)
    values = jnp.clip(jax.random.normal(key, (REQUESTS, PREFIX, KV_HEADS * HEAD_DIM)), -8.0, 8.0)
    return values.astype(jnp.bfloat16)


def draw_resid(key, part):
    key = jax.random.fold_in(key, 3)
    subkeys = jax.random.split(key, 3)
    values = jnp.clip(jax.random.normal(subkeys[0], (TOKENS, D)), -6.0, 6.0)
    row_scale = jnp.exp(jax.random.uniform(subkeys[1], (TOKENS, 1), minval=math.log(0.3), maxval=math.log(3.0)))
    column_scale = jnp.exp(jax.random.uniform(subkeys[2], (1, D), minval=math.log(0.6), maxval=math.log(1.6)))
    return (values * row_scale * column_scale).astype(jnp.bfloat16)


def place_ends(values, stream_key, smallest, high):
    dims = values.shape
    index_at = [jax.random.randint(jax.random.fold_in(stream_key, axis), (), 0, dims[axis]) for axis in range(len(dims))]
    values = values.at[tuple(index_at)].set(smallest)
    longest = dims.index(max(dims))
    index_at[longest] = (index_at[longest] + 1) % dims[longest]
    return values.at[tuple(index_at)].set(high)


def levels(stream_key, shape, shards, least, top_value):
    gain, own = 1.0, jax.random.fold_in(stream_key, 6)
    for axis_at, shards_of in shards:
        draws = jnp.exp(jax.random.uniform(jax.random.fold_in(own, axis_at), (shards_of,), jnp.float32, least / len(shards), top_value / len(shards)))
        gain = gain * jnp.repeat(draws, shape[axis_at] // shards_of).reshape([-1 if axis == axis_at else 1 for axis in range(len(shape))])
    return gain


def deal_out(stream_key, own, number, rows, amount, top, bound, lean):
    sequence = jax.random.permutation(stream_key, amount)
    crowded, usual = portions_of(amount, rows * top, bound, lean, True), portions_of(amount, rows * top, bound, lean, False)
    places = jnp.arange(amount)

    def named(lengths, turn):
        used = int((lengths > 0).sum())
        fixed = max(1, used // 4)
        passed = fixed + (places - fixed + turn * (used - fixed)) % max(1, amount - fixed)
        return jnp.zeros((amount,), jnp.int32).at[sequence[jnp.where(places < fixed, places, passed)]].set(jnp.asarray(lengths, jnp.int32))

    lengths = jnp.where(number % 4 == 0, named(crowded, number // 4), named(usual, number - number // 4 - 1))
    mixed = jax.random.permutation(jax.random.fold_in(own, 3), amount)
    source_of, taker = mixed[0:amount // 2 * 2:2], mixed[1:amount // 2 * 2:2]
    slack = jnp.minimum(lengths[source_of] - 1, bound - lengths[taker]) // 2
    slack = jnp.where((source_of == sequence[0]) | (taker == sequence[0]) | (lengths[taker] == 0), 0, jnp.maximum(slack, 0))
    passed = jax.random.randint(jax.random.fold_in(own, 4), (amount // 2,), 0, 1 << 20) % (slack + 1)
    lengths = lengths.at[source_of].add(-passed).at[taker].add(passed)
    labels = jnp.searchsorted(jnp.cumsum(lengths), jnp.arange(rows * top), side="right").astype(jnp.int32)
    grid = labels.reshape(top, rows).T
    grid = grid[jax.random.permutation(jax.random.fold_in(own, 1), rows)]
    turn = jax.random.randint(jax.random.fold_in(own, 2), (rows, 1), 0, top)
    return jnp.take_along_axis(grid, (jnp.arange(top)[None, :] + turn) % top, axis=1)


def portions_of(number_of, total, reach, slope, full):
    portions = [(1 << 20) // math.isqrt(standing ** slope) + 1 for standing in range(1, number_of + 1)]
    largest = reach if full else min(reach, max(-(-total // number_of), total * portions[0] // sum(portions)))
    least = 1 if total - largest >= number_of - 1 else 0
    given, rest = [largest] + [least] * (number_of - 1), total - largest - least * (number_of - 1)
    while rest > 0:
        free = [i for i in range(1, number_of) if given[i] < largest] or [i for i in range(1, number_of) if given[i] < reach]
        mass, remaining = sum([portions[i] for i in free]), rest
        for i in free:
            extra = min(reach - given[i], max(1, remaining * portions[i] // mass), rest)
            given[i] = given[i] + extra
            rest = rest - extra
    return np.array(given)


def centred(stream_key, shape, spread, most, shards=(), kind=jnp.bfloat16):
    values = spread * jax.random.normal(stream_key, shape, jnp.float32)
    if shards:
        values = values * levels(stream_key, shape, shards, -0.22, 0.18)
    return jnp.clip(values, -most, most).astype(kind)


def setup_inputs(seed: int = 0, part: int = 0) -> dict:
    key_of = jax.random.split(jax.random.key(seed), 14)
    part_keys = jax.random.split(jax.random.fold_in(key_of[13], part), 14)
    resid = draw_resid(jax.random.fold_in(jax.random.fold_in(key_of[13], part), 71), part)
    queries = draw_queries(jax.random.fold_in(jax.random.fold_in(key_of[13], part), 71), part)
    block_keys = centred(part_keys[2], (TOKENS, KV_HEADS * HEAD_DIM), 1.0, 6.0, ((0, 16),))
    block_values = centred(part_keys[3], (TOKENS, KV_HEADS * HEAD_DIM), 1.0, 6.0, ((0, 16),))
    cache_keys = draw_cache_keys(jax.random.fold_in(jax.random.fold_in(key_of[13], part), 71), part)
    cache_values = centred(part_keys[5], (REQUESTS, PREFIX, KV_HEADS * HEAD_DIM), 1.0, 6.0, ((0, 16),))
    prefix_len = place_ends(jax.random.randint(part_keys[6], (REQUESTS,), 2, PREFIX + 1), jax.random.fold_in(part_keys[6], 1), 2, PREFIX).astype(jnp.int32)
    norm_gain = jnp.clip(1.0 + 0.1 * jax.random.normal(key_of[7], (D,), jnp.float32), 0.5, 1.5)
    expert_ids_keys = jax.random.split(jax.random.fold_in(part_keys[8], 1), TOKENS // TOK_DEV)
    expert_ids_turns = jax.random.permutation(jax.random.fold_in(part_keys[8], 3), TOKENS // TOK_DEV)
    expert_ids = jax.vmap(lambda own, number: deal_out(jax.random.fold_in(part_keys[8], 2), own, number, TOK_DEV, EXPERTS, TOPK, CAP, 2))(expert_ids_keys, expert_ids_turns).reshape((TOKENS, TOPK))
    route_weights = jnp.clip(0.1 + 0.9 * jax.random.uniform(part_keys[9], (TOKENS, TOPK), jnp.float32) ** levels(part_keys[9], (TOKENS, TOPK), ((0, 16),), -0.2, 0.2), 0.1, 1.0)
    w_gate = centred(key_of[10], (2 * EXPERTS, D, FF // 2), D ** -0.5, 0.09375, ((0, 16),))
    w_up = centred(key_of[11], (2 * EXPERTS, D, FF // 2), D ** -0.5, 0.09375, ((0, 16),))
    w_down = centred(key_of[12], (2 * EXPERTS, FF // 2, D), FF ** -0.5, 0.25, ((0, 16),))
    return dict(resid=resid, queries=queries, block_keys=block_keys, block_values=block_values, cache_keys=cache_keys, cache_values=cache_values, prefix_len=prefix_len, norm_gain=norm_gain, expert_ids=expert_ids, route_weights=route_weights, w_gate=w_gate, w_up=w_up, w_down=w_down)


def attend_request(query_rows, own_keys, own_values, cached_keys, cached_values, prefix_length):
    groups = HEADS // KV_HEADS
    query_heads = query_rows.astype(jnp.float32).reshape(BLOCK, KV_HEADS, groups, HEAD_DIM)
    key_rows = jnp.concatenate([cached_keys, own_keys], 0).astype(jnp.float32).reshape(-1, KV_HEADS, HEAD_DIM)
    value_rows = jnp.concatenate([cached_values, own_values], 0).astype(jnp.float32).reshape(-1, KV_HEADS, HEAD_DIM)
    scores = jnp.einsum('ikgd,jkd->kgij', query_heads, key_rows) * HEAD_DIM ** (-0.5)
    position = jnp.arange(PREFIX + BLOCK, dtype=jnp.int32)
    usable = (position < prefix_length) | (position >= PREFIX)
    scores = jnp.where(usable, scores, jnp.float32(-1e+30))
    top_score = lax.optimization_barrier(jnp.max(scores, -1, keepdims=True))
    weights = jnp.exp(scores - top_score)
    probs = (weights / lax.optimization_barrier(jnp.sum(weights, -1, keepdims=True))).astype(jnp.bfloat16)
    mixed = jnp.einsum('kgij,jkd->ikgd', probs.astype(jnp.float32), value_rows)
    return mixed.reshape(BLOCK, HEADS * HEAD_DIM).astype(jnp.bfloat16)

def reference(resid, queries, block_keys, block_values, cache_keys, cache_values, prefix_len, norm_gain, expert_ids, route_weights, w_gate, w_up, w_down):

    def one_request(inputs):
        return attend_request(*inputs)
    attended = lax.map(one_request, (queries.reshape(REQUESTS, BLOCK, -1), block_keys.reshape(REQUESTS, BLOCK, -1), block_values.reshape(REQUESTS, BLOCK, -1), cache_keys, cache_values, prefix_len)).reshape(TOKENS, D)
    hidden = (resid.astype(jnp.float32) + attended.astype(jnp.float32)).astype(jnp.bfloat16)
    hidden_wide = hidden.astype(jnp.float32)
    normed = (hidden_wide * lax.rsqrt(lax.optimization_barrier(jnp.mean(hidden_wide * hidden_wide, -1, keepdims=True)) + 1e-06) * norm_gain.astype(jnp.float32)).astype(jnp.bfloat16)
    flat_ids = expert_ids.reshape(-1).astype(jnp.int32)
    flat_weights = route_weights.reshape(-1)
    token_of = (jnp.arange(TOKENS * TOPK, dtype=jnp.int32) // TOPK).astype(jnp.int32)
    most_rows = N_EXPERT * CAP

    def add_expert(accumulated, expert):
        chosen = flat_ids == expert
        picked = jnp.nonzero(chosen, size=most_rows, fill_value=0)[0].astype(jnp.int32)
        live_rows = jnp.arange(most_rows, dtype=jnp.int32) < jnp.sum(chosen.astype(jnp.int32))
        token_rows = token_of[picked]
        inputs = normed[token_rows]
        halves = []
        for which_half in range(2):
            slice_index = 2 * expert + which_half
            gate_out = jnp.dot(inputs, w_gate[slice_index], preferred_element_type=jnp.float32)
            upward = jnp.dot(inputs, w_up[slice_index], preferred_element_type=jnp.float32)
            active = (jax.nn.silu(gate_out) * upward).astype(jnp.bfloat16)
            halves.append(jnp.dot(active, w_down[slice_index], preferred_element_type=jnp.float32).astype(jnp.bfloat16))
        expert_out = (halves[0].astype(jnp.float32) + halves[1].astype(jnp.float32)).astype(jnp.bfloat16)
        scaled = jnp.where(live_rows, flat_weights[picked], jnp.float32(0.0))[:, None] * expert_out.astype(jnp.float32)
        return (accumulated.at[token_rows].add(scaled), None)
    accumulated, ignored = lax.scan(add_expert, jnp.zeros((TOKENS, D), jnp.float32), jnp.arange(EXPERTS, dtype=jnp.int32))
    return (hidden_wide + accumulated).astype(jnp.bfloat16)
```

```python
import jax
import jax.numpy as jnp
from jax import lax
from jax.experimental import pallas as pl
from jax.experimental.pallas import tpu as pltpu
from jax.sharding import PartitionSpec as P

HEADS = 32
KV_HEADS = 4
HEAD_DIM = 128
BLOCK = 32
GROUPS = HEADS // KV_HEADS
F32 = jnp.float32
BF16 = jnp.bfloat16


def attention_kernel(
    lens_ref, q_ref, bk_ref, bv_ref, ck_ref, cv_ref, resid_ref, gain_ref, hidden_ref, normed_ref
):
    request = pl.program_id(0)
    kv = pl.program_id(1)
    prefix = ck_ref.shape[1]
    length = lens_ref[request]
    q = q_ref[...]
    rows = jnp.concatenate([q[:, g * HEAD_DIM : (g + 1) * HEAD_DIM] for g in range(GROUPS)], 0)
    contract = (((1,), (1,)), ((), ()))
    scale = HEAD_DIM ** (-0.5)
    cached = lax.dot_general(rows, ck_ref[0], contract, preferred_element_type=F32) * scale
    own = lax.dot_general(rows, bk_ref[...], contract, preferred_element_type=F32) * scale
    position = lax.broadcasted_iota(jnp.int32, (1, prefix), 1)
    cached = jnp.where(position < length, cached, F32(-1e30))
    top = jnp.maximum(jnp.max(cached, -1, keepdims=True), jnp.max(own, -1, keepdims=True))
    cached = jnp.exp(cached - top)
    own = jnp.exp(own - top)
    total = jnp.sum(cached, -1, keepdims=True) + jnp.sum(own, -1, keepdims=True)
    mixed = jnp.dot(cached.astype(BF16), cv_ref[0], preferred_element_type=F32)
    mixed += jnp.dot(own.astype(BF16), bv_ref[...], preferred_element_type=F32)
    mixed = (mixed / total).astype(BF16)
    wide = GROUPS * HEAD_DIM
    attended = jnp.concatenate([mixed[g * BLOCK : (g + 1) * BLOCK] for g in range(GROUPS)], 1)
    columns = pl.ds(pl.multiple_of(kv * wide, wide), wide)
    hidden_ref[:, columns] = (
        resid_ref[:, columns].astype(F32) + attended.astype(F32)
    ).astype(BF16)

    @pl.when(kv == KV_HEADS - 1)
    def _():
        hidden = hidden_ref[...].astype(F32)
        normed_ref[...] = (
            hidden
            * lax.rsqrt(jnp.mean(hidden * hidden, -1, keepdims=True) + 1e-06)
            * gain_ref[...]
        ).astype(BF16)


def attend(resid, queries, block_keys, block_values, cache_keys, cache_values, prefix_len, gain):
    requests, prefix, _ = cache_keys.shape
    width = resid.shape[1]
    wide = GROUPS * HEAD_DIM
    rows_kv = pl.BlockSpec((BLOCK, HEAD_DIM), lambda r, k, lens: (r, k))
    cached = pl.BlockSpec((1, prefix, HEAD_DIM), lambda r, k, lens: (r, 0, k))
    whole = pl.BlockSpec((BLOCK, width), lambda r, k, lens: (r, 0))
    return pl.pallas_call(
        attention_kernel,
        grid_spec=pltpu.PrefetchScalarGridSpec(
            num_scalar_prefetch=1,
            grid=(requests, KV_HEADS),
            in_specs=[
                pl.BlockSpec((BLOCK, wide), lambda r, k, lens: (r, k)),
                rows_kv,
                rows_kv,
                cached,
                cached,
                whole,
                pl.BlockSpec((1, width), lambda r, k, lens: (0, 0)),
            ],
            out_specs=[whole, whole],
        ),
        out_shape=[jax.ShapeDtypeStruct(resid.shape, BF16)] * 2,
        compiler_params=pltpu.CompilerParams(vmem_limit_bytes=48 << 20),
        name="attention",
    )(prefix_len, queries, block_keys, block_values, cache_keys, cache_values, resid, gain[None, :])


def ffn(rows, weights):
    total = None
    for gate, up, down in weights:
        gate_out = jnp.dot(rows, gate, preferred_element_type=F32)
        upward = jnp.dot(rows, up, preferred_element_type=F32)
        active = (jax.nn.silu(gate_out) * upward).astype(BF16)
        part = jnp.dot(active, down, preferred_element_type=F32)
        total = part if total is None else total + part
    return total


def route_table(expert_ids, route_weights, experts):
    onehot = (expert_ids[:, :, None] == jnp.arange(experts, dtype=jnp.int32)).astype(F32)
    weight = jnp.sum(onehot * route_weights[:, :, None], 1)
    return jnp.concatenate([weight, jnp.sum(onehot, 1)], 1)


def pick_rows(mask, capacity):
    tokens = mask.shape[-1]
    order = jnp.arange(tokens, dtype=jnp.int32)
    before = (order[:, None] < order[None, :]).astype(F32)
    rank = jnp.dot(mask, before, preferred_element_type=F32)
    slot = jnp.arange(capacity, dtype=jnp.int32).astype(F32)
    return (rank[:, None, :] == slot[None, :, None]).astype(F32) * mask[:, None, :]


def pairs(step, flip, valid):
    found = []
    for z in range(4):
        for y in range(2):
            for c in range(2):
                to = step(z)
                if valid(z) and 0 <= to < 4:
                    found.append((4 * z + 2 * y + c, 4 * to + 2 * (y ^ flip) + c))
    return found


def always(z):
    return True


def ends(z):
    return z in (0, 3)


def middle(z):
    return z in (1, 2)


def send(value, step, flip, valid):
    return lax.ppermute(value, "expert", pairs(step, flip, valid))


def stay(z):
    return z


def plus(z):
    return z + 1


def minus(z):
    return z - 1


def grid_moe(hidden, normed, expert_ids, route_weights, weights, topk):
    position = lax.axis_index("expert")
    z, y = position // 4, (position // 2) % 2
    experts = 8
    tokens, width = normed.shape
    capacity = 2 * ((3 * tokens * topk + 4 * experts - 1) // (4 * experts))
    groups = [[2 * chip + core for chip in range(8)] for core in range(2)]
    table = lax.all_gather(
        route_table(expert_ids, route_weights, experts), "expert", axis_index_groups=groups
    )
    near = jnp.where(z == 0, 1, z - 1)
    late = jnp.where(z == 0, 3, jnp.where(z == 3, 0, z + 1))
    sources = jnp.stack([z, near, z ^ 2, late])
    mine = jnp.take(table, 2 * sources + y, axis=0)
    theirs = jnp.take(table, 2 * sources + 1 - y, axis=0)
    here, across = 2 * z + y, 2 * z + 1 - y

    def column(values, index):
        return lax.dynamic_index_in_dim(values, index, 2, keepdims=False)

    picks = pick_rows(column(mine, experts + across), capacity).astype(BF16)
    own_weight = column(mine, here)
    arriving = pick_rows(column(theirs, experts + here), capacity)
    cross_weight = jnp.sum(arriving * column(theirs, here)[:, None, :], 2)

    def pick(slot, rows):
        return jnp.dot(picks[slot], rows, preferred_element_type=F32).astype(BF16)

    def place(slot, rows):
        return jnp.dot(picks[slot].T, rows, preferred_element_type=F32)

    is_end = (z == 0) | (z == 3)
    up1 = send(normed, plus, 0, always)
    down1 = send(normed, minus, 0, always)
    cross0 = send(pick(0, normed), stay, 1, always)
    up2 = send(up1, plus, 0, lambda z: z >= 1)
    down2 = send(down1, minus, 0, lambda z: z <= 2)
    row_near = jnp.where(z == 0, down1, up1)
    cross_near = send(pick(1, row_near), stay, 1, always)
    cross_mid = send(pick(3, down1), stay, 1, middle)
    row_two = jnp.where(z >= 2, up2, down2)
    far = lax.ppermute(row_two, "expert", pairs(lambda z: {1: 0, 2: 3}.get(z, -1), 0, middle))
    cross_two = send(pick(2, row_two), stay, 1, always)
    cross_end = send(pick(3, far), stay, 1, ends)
    row_late = jnp.where(is_end, far, down1)
    cross_late = jnp.where(is_end, cross_end, cross_mid)

    rows = jnp.concatenate(
        [normed, row_near, row_two, row_late, cross0, cross_near, cross_two, cross_late], 0
    )
    scale = jnp.concatenate([own_weight.reshape(-1), cross_weight.reshape(-1)])
    out = (ffn(rows, weights) * scale[:, None]).astype(BF16)
    mine_out = [out[i * tokens : (i + 1) * tokens].astype(F32) for i in range(4)]
    base = 4 * tokens
    cross_out = [out[base + i * capacity : base + (i + 1) * capacity] for i in range(4)]

    back_end = send(cross_out[3], stay, 1, ends)
    back_two = send(cross_out[2], stay, 1, always)
    sum_far = mine_out[3] + place(3, back_end)
    got_far = lax.ppermute(
        sum_far.astype(BF16), "expert", pairs(lambda z: {0: 1, 3: 2}.get(z, -1), 0, ends)
    )
    sum_two = (mine_out[2] + place(2, back_two) + got_far.astype(F32)).astype(BF16)
    got_down = send(sum_two, minus, 0, lambda z: z >= 2)
    got_up = send(sum_two, plus, 0, lambda z: z <= 1)
    back_near = send(cross_out[1], stay, 1, always)
    back_mid = send(cross_out[3], stay, 1, middle)
    sum_near = (mine_out[1] + place(1, back_near) + got_down.astype(F32)).astype(BF16)
    sum_next = (mine_out[3] + place(3, back_mid) + got_up.astype(F32)).astype(BF16)
    last_up = send(jnp.where(z == 0, sum_near, sum_next), plus, 0, always)
    last_down = send(sum_near, minus, 0, always)
    back0 = send(cross_out[0], stay, 1, always)
    return (
        hidden.astype(F32)
        + mine_out[0]
        + place(0, back0)
        + last_up.astype(F32)
        + last_down.astype(F32)
    ).astype(BF16)


def gathered_moe(hidden, normed, expert_ids, route_weights, weights, topk):
    devices = lax.axis_size("expert")
    position = lax.axis_index("expert")
    chips = devices // 2
    groups = [[2 * chip + core for chip in range(chips)] for core in range(2)]
    table = lax.all_gather(
        route_table(expert_ids, route_weights, chips),
        "expert",
        tiled=True,
        axis_index_groups=groups,
    )
    rows = lax.all_gather(normed, "expert", tiled=True, axis_index_groups=groups)
    scale = lax.dynamic_index_in_dim(table, position // 2, 1)
    out = (ffn(rows, weights) * scale).astype(BF16)
    mixture = lax.psum_scatter(
        out, "expert", scatter_dimension=0, tiled=True, axis_index_groups=groups
    )
    return (hidden.astype(F32) + mixture.astype(F32)).astype(BF16)


def local(
    resid,
    queries,
    block_keys,
    block_values,
    cache_keys,
    cache_values,
    prefix_len,
    norm_gain,
    expert_ids,
    route_weights,
    w_gate,
    w_up,
    w_down,
):
    devices = lax.axis_size("expert")
    swap = [(device, device ^ 1) for device in range(devices)]
    held = (w_gate[0], w_up[0], w_down[0])
    other = tuple(lax.ppermute(part, "expert", swap) for part in held)
    hidden, normed = attend(
        resid,
        queries,
        block_keys,
        block_values,
        cache_keys,
        cache_values,
        prefix_len,
        norm_gain,
    )
    moe = grid_moe if devices == 16 else gathered_moe
    return moe(
        hidden, normed, expert_ids, route_weights, (held, other), expert_ids.shape[1]
    )


def solution(mesh):
    rows = P(("group", "expert"), None)
    cube = P(("group", "expert"), None, None)
    slices = P("expert", None, None)
    placed = (
        rows,
        rows,
        rows,
        rows,
        cube,
        cube,
        P(("group", "expert")),
        P(),
        rows,
        rows,
        slices,
        slices,
        slices,
    )
    return jax.shard_map(local, mesh=mesh, in_specs=placed, out_specs=rows, check_vma=False)
```
